32 devices in a mesh: groups: 2 (over y), wide: 4 (over z), narrow: 2 (over x), inner: 2 (over core).
Axes of the slice: x: 2, y: 2, z: 4, core: 2. Of those that a mesh axis runs over, the one named last changes fastest.
Arguments:
- centres: bfloat16 [12288, 768], P(('groups', 'wide', 'narrow')), parts along dimension 0, may hold values from -6 to 6
- weights: float32 [12288, 1000], P(('groups', 'wide', 'narrow'), 'inner'), parts along dimension 0, may hold values from -0.625 to 0.625
- pool_points: bfloat16 [1024, 768], P(('groups', 'wide', 'narrow')), parts along dimension 0, may hold values from -6 to 6
- pool_labels: bfloat16 [1024, 1000], P(('groups', 'wide', 'narrow'), 'inner'), parts along dimension 0, may hold values from -6 to 6
- batch_index: int32 [8, 8], P('groups', ('wide', 'narrow')), parts along dimension 0, may hold values from 0 to 63
- landmark_index: int32 [8192], P(('groups', 'wide', 'narrow')), parts along dimension 0, may hold values from 0 to 767
- eigvecs: float32 [8192, 160], P(('groups', 'wide', 'narrow')), parts along dimension 0, may hold values from -0.09375 to 0.09375
- eig_scale: float32 [320], P('groups'), parts along dimension 0, may hold values from 2 to 20
Outputs:
- descent: float32 [12288, 1000], P(('groups', 'wide', 'narrow'), 'inner'), parts along dimension 0
- residual: float32 [16, 1000], P('groups', 'inner'), parts along dimension 0
The draws below stay inside these ranges and needn't reach their ends.
There are 2 independent parts, one for each index of `groups`. The reference program is written for one: setup_inputs(seed, part) draws one part's arguments, and reference() takes and returns one part's arrays. A program takes and returns all parts, laid end to end along the dimension named above; each array names one. Nothing has to cross between parts.
All inputs are finite; a program needn't handle non-finite values.
Results may differ from the reference program's by a relative error of at most 0.0003.
Values may be sent and summed in bfloat16 or wider, within the bound.
A program may use at most 64 MiB of HBM per device.

```python
import math
import jax
import jax.numpy as jnp
from jax import lax

D = 768
OUT = 1000
EIGS = 160
STEPS = 4
LM_DEV = 512
CDEV = 768
POOL_DEV = 64
PTS_DEV = 1
CENTRES = 6144
LANDMARKS = 4096
POOL = 512
BATCH = 8


def touch_ends(drawn, stream_key, least, high):
    place = [jax.random.randint(jax.random.fold_in(stream_key, axis), (), 0, length) for axis, length in enumerate(drawn.shape)]
    longest = drawn.shape.index(max(drawn.shape))
    beside = place[:longest] + [(place[longest] + 1) % drawn.shape[longest]] + place[longest + 1:]
    return drawn.at[tuple(place)].set(least).at[tuple(beside)].set(high)


def level_of(key, dims, shards, smallest, top_value):
    def one(position, blocks):
        draws = jax.random.uniform(jax.random.fold_in(jax.random.fold_in(key, 6), position), (blocks,), jnp.float32, smallest / len(shards), top_value / len(shards))
        return jnp.repeat(jnp.exp(draws), dims[position] // blocks).reshape((-1,) + (1,) * (len(dims) - position - 1))

    level = one(*shards[0])
    for cut in shards[1:]:
        level = level * one(*cut)
    return level


def bell_draw(key, shape, scale, most, cuts=(), held_as=jnp.bfloat16):
    gain = level_of(key, shape, cuts, -0.22, 0.18) if cuts else 1.0
    drawn = jax.random.normal(key, shape, jnp.float32) * scale * gain
    return jnp.minimum(jnp.maximum(drawn, -most), most).astype(held_as)


def setup_inputs(seed: int = 0, part: int = 0) -> dict:
    streams_of = jax.random.split(jax.random.key(seed), 9)
    part_splits = jax.random.split(jax.random.fold_in(streams_of[8], part), 9)
    centres = bell_draw(part_splits[0], (CENTRES, D), 1.0, 6.0, ((0, 8),))
    weights = bell_draw(part_splits[1], (CENTRES, OUT), (CENTRES // 64) ** -0.5, 0.625, ((0, 8), (1, 2)), jnp.float32)
    pool_points = bell_draw(part_splits[2], (POOL, D), 1.0, 6.0, ((0, 8),))
    pool_labels = bell_draw(part_splits[3], (POOL, OUT), 1.0, 6.0, ((0, 8), (1, 2)))
    batch_index = touch_ends(jax.random.randint(part_splits[4], (STEPS, BATCH), 0, POOL_DEV), jax.random.fold_in(part_splits[4], 1), 0, POOL_DEV - 1).astype(jnp.int32)
    landmark_index = touch_ends(jax.random.randint(part_splits[5], (LANDMARKS,), 0, CDEV), jax.random.fold_in(part_splits[5], 1), 0, CDEV - 1).astype(jnp.int32)
    eigvecs = bell_draw(part_splits[6], (LANDMARKS, EIGS), LANDMARKS ** -0.5, 0.09375, ((0, 8),), jnp.float32)
    eig_scale = jnp.clip(jnp.exp(jax.random.uniform(part_splits[7], (EIGS,), jnp.float32, math.log(2.0), math.log(20.0))), 2.0, 20.0)
    return dict(centres=centres, weights=weights, pool_points=pool_points, pool_labels=pool_labels, batch_index=batch_index, landmark_index=landmark_index, eigvecs=eigvecs, eig_scale=eig_scale)


def squared_norms(points):
    widened = points.astype(jnp.float32)
    return lax.optimization_barrier(jnp.sum(widened * widened, axis=1))

def kernel_block(centre_rows, centre_norms, batch_points, batch_norms, spread):
    dot_terms = lax.dot_general(centre_rows, batch_points, (((1,), (1,)), ((), ())), preferred_element_type=jnp.float32)
    squared = centre_norms[:, None] + batch_norms[None, :] - 2.0 * dot_terms
    return jnp.exp(-jnp.sqrt(squared) / spread)

def reference(centres, weights, pool_points, pool_labels, batch_index, landmark_index, eigvecs, eig_scale):
    spread = math.sqrt(0.5 * D)
    step_size = 32.0 / (CENTRES * BATCH)
    centre_norms = squared_norms(centres)
    landmark_rows = jnp.arange(LANDMARKS, dtype=jnp.int32) // LM_DEV * CDEV + landmark_index.astype(jnp.int32)
    owner_rows = jnp.arange(BATCH, dtype=jnp.int32) // PTS_DEV * POOL_DEV
    descent = jnp.zeros(weights.shape, jnp.float32)
    residual = jnp.zeros((BATCH, OUT), jnp.float32)
    for step_index in range(STEPS):
        picked = owner_rows + batch_index[step_index].astype(jnp.int32)
        batch_points = pool_points[picked]
        batch_labels = pool_labels[picked].astype(jnp.float32)
        kernel = kernel_block(centres, centre_norms, batch_points, squared_norms(batch_points), spread)
        predicted = lax.dot_general(kernel, weights, (((0,), (0,)), ((), ())), precision=lax.Precision.HIGHEST, preferred_element_type=jnp.float32)
        residual = predicted - batch_labels
        gradient = jnp.dot(kernel, residual, precision=lax.Precision.HIGHEST, preferred_element_type=jnp.float32)
        at_landmarks = gradient[landmark_rows]
        coefficients = lax.dot_general(eigvecs, at_landmarks, (((0,), (0,)), ((), ())), precision=lax.Precision.HIGHEST, preferred_element_type=jnp.float32)
        correction_rows = jnp.dot(eigvecs, eig_scale[:, None] * coefficients, precision=lax.Precision.HIGHEST, preferred_element_type=jnp.float32)
        correction = gradient.at[landmark_rows].add(-correction_rows)
        weights = weights - step_size * correction
        descent = descent + correction
    return (descent, residual)
```

```python
import functools
import math

import jax
import jax.numpy as jnp
from jax import lax
from jax.experimental import pallas as pl
from jax.experimental.pallas import tpu as pltpu
from jax.sharding import PartitionSpec as P

MESH = pl.DeviceIdType.MESH
F32, BF16, I32 = jnp.float32, jnp.bfloat16, jnp.int32
LANES = 128
ROWS_PER_STEP = 8
VMEM_BYTES = 40 * 1024 * 1024

NN = (((1,), (0,)), ((), ()))
NT = (((1,), (1,)), ((), ()))
TN = (((0,), (0,)), ((), ()))


def dot(a, b, dims):
    return lax.dot_general(a, b, dims, preferred_element_type=F32)


def split(x):
    head = x.astype(BF16)
    return head, (x - head.astype(F32)).astype(BF16)


def dot_split(a_parts, b_parts, dims):
    a_head, a_rest = a_parts
    b_head, b_rest = b_parts
    rows = a_head.shape[0]
    both = dot(jnp.concatenate([a_head, a_rest], axis=0), b_head, dims)
    return both[:rows] + (both[rows:] + dot(a_head, b_rest, dims))


def iota(shape, dim):
    return lax.broadcasted_iota(I32, shape, dim)


def steps_kernel(
    narrow, shards, steps, spread, step_size,
    bidx_ref, lidx_hbm, scale_hbm, centres_hbm, weights_hbm, pool_hbm, labels_hbm, eig_hbm,
    mt_ref, r_ref,
    lidx, scale, centres, weights, pool, labels, eig,
    w_head, w_rest, e_head, e_rest,
    own_pts, all_pts, x, x_in, ag,
    load_sem, pts_send, pts_recv, x_send, x_recv, ag_send, ag_recv,
):
    me = lax.axis_index("wide") * narrow + lax.axis_index("narrow")
    peers = [lax.rem(me + k, shards) for k in range(1, shards)]

    def at(peer):
        return {"wide": peer // narrow, "narrow": lax.rem(peer, narrow)}

    barrier = pltpu.get_barrier_semaphore()
    for peer in peers:
        pl.semaphore_signal(barrier, inc=1, device_id=at(peer), device_id_type=MESH)

    loads = {}
    for place, (name, src, dst) in enumerate((
        ("pool", pool_hbm, pool),
        ("lidx", lidx_hbm, lidx),
        ("eig", eig_hbm, eig),
        ("centres", centres_hbm, centres),
        ("labels", labels_hbm, labels),
        ("scale", scale_hbm, scale),
        ("weights", weights_hbm, weights),
    )):
        loads[name] = pltpu.make_async_copy(src, dst, load_sem.at[place])
        loads[name].start()

    total = steps * shards
    count, width = centres.shape
    outs = weights.shape[1]
    eigs = eig.shape[1]
    pool_rows = pool.shape[0]
    pieces = width // LANES
    half = x.shape[2]
    w_cols = 2 * half - 256
    b_col = w_cols + eigs - half

    loads["pool"].wait()
    stacked = jnp.concatenate(
        [pool[:, LANES * q:LANES * (q + 1)] for q in range(pieces)], axis=0
    )
    pack_rows = own_pts.shape[0]
    shape = (pack_rows, pieces * pool_rows)
    row, col = iota(shape, 0), iota(shape, 1)
    wanted = row // steps * pool_rows
    step_of = row % steps
    for s in range(steps):
        wanted = wanted + jnp.where(step_of == s, bidx_ref[0, s], 0)
    own = dot(jnp.where(row // steps < pieces, jnp.where(col == wanted, 1.0, 0.0), 0.0).astype(BF16), stacked, NN)
    own_pts[...] = own.astype(BF16)

    pl.semaphore_wait(barrier, shards - 1)
    pts_copies = []
    for peer in peers:
        copy = pltpu.make_async_remote_copy(
            src_ref=own_pts, dst_ref=all_pts.at[me],
            send_sem=pts_send.at[peer], recv_sem=pts_recv.at[me],
            device_id=at(peer), device_id_type=MESH,
        )
        copy.start()
        pts_copies.append(copy)
    all_pts[pl.ds(me, 1)] = own_pts[...][None]
    x[...] = jnp.zeros_like(x)

    loads["lidx"].wait()
    loads["eig"].wait()
    marks = lidx.shape[1]
    chosen = jnp.where(iota((count, marks), 0) == lidx[...], 1.0, 0.0).astype(BF16)
    eig_head, eig_rest = split(eig[...])
    placed = dot(chosen, eig_head, NN) + dot(chosen, eig_rest, NN)
    e_parts = split(placed)
    e_head[...], e_rest[...] = e_parts

    loads["centres"].wait()
    sums = jnp.zeros((count, LANES), F32)
    for q in range(pieces):
        piece = centres[:, LANES * q:LANES * (q + 1)].astype(F32)
        sums = sums + piece * piece
    s_head, s_rest = split(sums)
    s_tail = (sums - s_head.astype(F32) - s_rest.astype(F32)).astype(BF16)
    ones = jnp.ones((16, LANES), BF16)
    centre_norms = (dot(ones, s_head, NT) + (dot(ones, s_rest, NT) + dot(ones, s_tail, NT)))[0:1]

    loads["labels"].wait()
    shape = (total, pool_rows)
    row, col = iota(shape, 0), iota(shape, 1)
    wanted = jnp.zeros(shape, I32)
    for s in range(steps):
        wanted = wanted + jnp.where(row // shards == s, bidx_ref[0, s], 0)
    pick = jnp.where(row % shards == me, jnp.where(col == wanted, 1.0, 0.0), 0.0).astype(BF16)
    label_rows = dot(pick, labels[...], NN)

    loads["scale"].wait()
    loads["weights"].wait()
    w_parts = split(weights[...])
    w_head[...], w_rest[...] = w_parts

    shape = (pieces * total, shards * pack_rows)
    row, col = iota(shape, 0), iota(shape, 1)
    source = row % shards * pack_rows + row // total * steps + row % total // shards
    order = jnp.where(col == source, 1.0, 0.0).astype(BF16)

    for copy in pts_copies:
        copy.wait_send()
    for peer in peers:
        pltpu.make_async_remote_copy(
            src_ref=own_pts, dst_ref=all_pts.at[peer],
            send_sem=pts_send.at[peer], recv_sem=pts_recv.at[peer],
            device_id=at(peer), device_id_type=MESH,
        ).wait_recv()
    ordered = dot(order, all_pts[...].reshape(shards * pack_rows, LANES), NN)
    points = jnp.concatenate([ordered[total * q:total * (q + 1)] for q in range(pieces)], axis=1)
    point_norms = jnp.sum(points * points, axis=1, keepdims=True)
    dots = dot(points.astype(BF16), centres[...], NT)
    squared = jnp.maximum(centre_norms + point_norms - 2.0 * dots, 0.0)
    kernel = jnp.exp(jnp.sqrt(squared) * (-1.0 / spread))

    k_parts = split(kernel)
    x_w = dot_split(k_parts, (w_head[...], w_rest[...]), NN) - label_rows
    x_e = dot_split(k_parts, (e_head[...], e_rest[...]), NN)
    x_k = dot_split(k_parts, k_parts, NT)
    for s in range(steps):
        rows = slice(shards * s, shards * (s + 1))
        x[2 * s] = x_w[rows, :half]
        x[2 * s + 1, :, :outs - half] = x_w[rows, half:]
        x[2 * s + 1, :, w_cols - half:b_col] = x_e[rows]
        x[2 * s + 1, :, b_col:b_col + total] = x_k[rows]

    x_copies = []
    for peer in peers:
        copy = pltpu.make_async_remote_copy(
            src_ref=x.at[peer], dst_ref=x_in.at[me],
            send_sem=x_send.at[peer], recv_sem=x_recv.at[me],
            device_id=at(peer), device_id_type=MESH,
        )
        copy.start()
        x_copies.append(copy)
    summed = x[pl.ds(me, 1)][0]
    for peer in peers:
        pltpu.make_async_remote_copy(
            src_ref=x.at[peer], dst_ref=x_in.at[peer],
            send_sem=x_send.at[peer], recv_sem=x_recv.at[peer],
            device_id=at(peer), device_id_type=MESH,
        ).wait_recv()
        summed = summed + x_in[pl.ds(peer, 1)][0]
    ag[pl.ds(me, 1)] = summed[None]
    ag_copies = []
    for peer in peers:
        copy = pltpu.make_async_remote_copy(
            src_ref=ag.at[me], dst_ref=ag.at[me],
            send_sem=ag_send.at[peer], recv_sem=ag_recv.at[me],
            device_id=at(peer), device_id_type=MESH,
        )
        copy.start()
        ag_copies.append(copy)
    for copy in x_copies:
        copy.wait_send()
    for peer in peers:
        pltpu.make_async_remote_copy(
            src_ref=ag.at[peer], dst_ref=ag.at[peer],
            send_sem=ag_send.at[peer], recv_sem=ag_recv.at[peer],
            device_id=at(peer), device_id_type=MESH,
        ).wait_recv()
    for copy in ag_copies:
        copy.wait_send()

    left = [ag[2 * s] for s in range(steps)]
    right = [ag[2 * s + 1] for s in range(steps)]
    rights = jnp.concatenate(right, axis=0)
    coeffs = rights[:, w_cols - half:b_col]
    gram = rights[:, b_col:b_col + total]
    scaled = split(coeffs * scale[...])
    coupling = (gram - dot_split(scaled, split(coeffs), NT)) * step_size
    mt_ref[...] = kernel - dot_split(scaled, (e_head[...], e_rest[...]), NT)

    rests = [
        jnp.concatenate([left[s], right[s][:, :w_cols - half]], axis=1) for s in range(steps)
    ]
    for s in range(steps):
        known = rests[s]
        for later in range(s + 1, steps):
            factors = coupling[shards * later:shards * (later + 1), shards * s:shards * (s + 1)]
            moved = rests[later]
            for j in range(shards):
                moved = moved - factors[:, j:j + 1] * known[j:j + 1, :]
            rests[later] = moved
        r_ref[shards * s:shards * (s + 1), :] = known


def apply_kernel(outs, last, mt_ref, r_ref, descent_ref, residual_ref):
    m_head, m_rest = split(mt_ref[...])
    r_all = r_ref[...][:, :outs]
    r_head, r_rest = split(r_all)
    lhs = jnp.concatenate([m_head, m_rest, m_head], axis=0)
    rhs = jnp.concatenate([r_head, r_head, r_rest], axis=0)
    descent_ref[...] = dot(lhs, rhs, TN)
    residual_ref[...] = r_all[last:]


def fused_body(
    narrow, shards,
    centres, weights, pool_points, pool_labels, batch_index, landmark_index, eigvecs, eig_scale
):
    steps = batch_index.shape[0]
    count, width = centres.shape
    outs = weights.shape[1]
    marks, eigs = eigvecs.shape
    pool_rows = pool_points.shape[0]
    spread = math.sqrt(0.5 * width)
    step_size = 32.0 / (count * shards * shards)
    total = steps * shards
    padded = -(-outs // LANES) * LANES
    half = (padded + 256) // 2
    pack_rows = -(-(steps * width // LANES) // 16) * 16
    any_spec = pl.BlockSpec(memory_space=pl.ANY)
    vmem_spec = pl.BlockSpec(memory_space=pltpu.VMEM)
    mt, r = pl.pallas_call(
        functools.partial(steps_kernel, narrow, shards, steps, spread, step_size),
        out_shape=(
            jax.ShapeDtypeStruct((total, count), F32),
            jax.ShapeDtypeStruct((total, padded), F32),
        ),
        in_specs=[pl.BlockSpec(memory_space=pltpu.SMEM)] + [any_spec] * 7,
        out_specs=(vmem_spec, vmem_spec),
        scratch_shapes=[
            pltpu.VMEM((1, marks), I32),
            pltpu.VMEM((1, eigs), F32),
            pltpu.VMEM((count, width), BF16),
            pltpu.VMEM((count, outs), F32),
            pltpu.VMEM((pool_rows, width), BF16),
            pltpu.VMEM((pool_rows, outs), BF16),
            pltpu.VMEM((marks, eigs), F32),
            pltpu.VMEM((count, outs), BF16),
            pltpu.VMEM((count, outs), BF16),
            pltpu.VMEM((count, eigs), BF16),
            pltpu.VMEM((count, eigs), BF16),
            pltpu.VMEM((pack_rows, LANES), BF16),
            pltpu.VMEM((shards, pack_rows, LANES), BF16),
            pltpu.VMEM((shards, ROWS_PER_STEP, half), F32),
            pltpu.VMEM((shards, ROWS_PER_STEP, half), F32),
            pltpu.VMEM((shards, ROWS_PER_STEP, half), F32),
            pltpu.SemaphoreType.DMA((7,)),
        ] + [pltpu.SemaphoreType.DMA((shards,))] * 6,
        compiler_params=pltpu.CompilerParams(
            collective_id=0, has_side_effects=True, vmem_limit_bytes=VMEM_BYTES
        ),
    )(
        batch_index.reshape(1, steps), landmark_index.reshape(1, marks),
        eig_scale.reshape(1, eigs), centres, weights, pool_points, pool_labels, eigvecs,
    )
    block = count // 3 if count % 384 == 0 else count
    return pl.pallas_call(
        functools.partial(apply_kernel, outs, total - shards),
        grid=(count // block,),
        out_shape=(
            jax.ShapeDtypeStruct((count, outs), F32),
            jax.ShapeDtypeStruct((shards, outs), F32),
        ),
        in_specs=[
            pl.BlockSpec((total, block), lambda i: (0, i)),
            pl.BlockSpec((total, padded), lambda i: (0, 0)),
        ],
        out_specs=(
            pl.BlockSpec((block, outs), lambda i: (i, 0)),
            pl.BlockSpec((shards, outs), lambda i: (0, 0)),
        ),
        compiler_params=pltpu.CompilerParams(vmem_limit_bytes=VMEM_BYTES),
    )(mt, r)


def plain_body(
    centres, weights, pool_points, pool_labels, batch_index, landmark_index, eigvecs, eig_scale
):
    axes = ("wide", "narrow")
    shards = lax.axis_size(axes)
    me = lax.axis_index(axes)
    steps, per_device = batch_index.shape
    batch = shards * per_device
    count, width = centres.shape
    outs = weights.shape[1]
    spread = math.sqrt(0.5 * width)
    step_size = 32.0 / (count * shards * batch)
    exact = functools.partial(
        lax.dot_general, precision=lax.Precision.HIGHEST, preferred_element_type=F32
    )
    own_points = jnp.take(pool_points, batch_index, axis=0)
    own_labels = jnp.take(pool_labels, batch_index, axis=0)
    points = lax.all_gather(own_points, axes, axis=1, tiled=True).reshape(steps * batch, width)
    wide_points = points.astype(F32)
    wide_centres = centres.astype(F32)
    point_norms = jnp.sum(wide_points * wide_points, axis=1, keepdims=True)
    centre_norms = jnp.sum(wide_centres * wide_centres, axis=1)[None]
    squared = centre_norms + point_norms - 2.0 * dot(points, centres, NT)
    kernel = jnp.exp(-jnp.sqrt(jnp.maximum(squared, 0.0)) / spread)
    placed = jnp.zeros((count, eigvecs.shape[1]), F32).at[landmark_index].add(eigvecs)
    labels = lax.dynamic_update_slice(
        jnp.zeros((steps, batch, outs), F32), own_labels.astype(F32), (0, me * per_device, 0)
    )
    predicted = exact(kernel, weights, NN) - labels.reshape(steps * batch, outs)
    predicted, coeffs, gram = lax.psum(
        (predicted, exact(kernel, placed, NN), exact(kernel, kernel, NT)), axes
    )
    scaled = coeffs * eig_scale[None]
    coupling = (gram - exact(scaled, coeffs, NT)) * step_size
    mixed = kernel - exact(scaled, placed, NT)
    known = predicted[:batch]
    for s in range(1, steps):
        rows = slice(batch * s, batch * (s + 1))
        fresh = predicted[rows] - exact(coupling[rows, :batch * s], known, NN)
        known = jnp.concatenate([known, fresh], axis=0)
    return exact(mixed, known, TN), known[-batch:]


def solution(mesh):
    narrow = mesh.shape["narrow"]
    shards = mesh.shape["wide"] * narrow

    def body(*args):
        centres, weights = args[0], args[1]
        steps, per_device = args[4].shape
        fits = (
            shards == ROWS_PER_STEP and 2 * steps == shards and per_device == 1
            and centres.shape[1] % LANES == 0 and args[6].shape[1] + steps * shards <= 256
        )
        if fits:
            return fused_body(narrow, shards, *args)
        return plain_body(*args)

    return jax.shard_map(
        body,
        mesh=mesh,
        in_specs=(
            P(("groups", "wide", "narrow"), None),
            P(("groups", "wide", "narrow"), "inner"),
            P(("groups", "wide", "narrow"), None),
            P(("groups", "wide", "narrow"), "inner"),
            P("groups", ("wide", "narrow")),
            P(("groups", "wide", "narrow")),
            P(("groups", "wide", "narrow"), None),
            P("groups"),
        ),
        out_specs=(P(("groups", "wide", "narrow"), "inner"), P("groups", "inner")),
        check_vma=False,
    )
```

```python
import functools
import math

import jax
import jax.numpy as jnp
from jax import lax
from jax.experimental import pallas as pl
from jax.experimental.pallas import tpu as pltpu
from jax.sharding import PartitionSpec as P

MESH = pl.DeviceIdType.MESH
F32, BF16, I32 = jnp.float32, jnp.bfloat16, jnp.int32
LANES = 128
ROWS_PER_STEP = 8
VMEM_BYTES = 60 * 1024 * 1024

NN = (((1,), (0,)), ((), ()))
NT = (((1,), (1,)), ((), ()))
TN = (((0,), (0,)), ((), ()))


def dot(a, b, dims):
    return lax.dot_general(a, b, dims, preferred_element_type=F32)


def split(x):
    head = x.astype(BF16)
    return head, (x - head.astype(F32)).astype(BF16)


def dot_split(a_parts, b_parts, dims):
    a_head, a_rest = a_parts
    b_head, b_rest = b_parts
    rows = a_head.shape[0]
    both = dot(jnp.concatenate([a_head, a_rest], axis=0), b_head, dims)
    return both[:rows] + (both[rows:] + dot(a_head, b_rest, dims))


def iota(shape, dim):
    return lax.broadcasted_iota(I32, shape, dim)


def steps_kernel(
    narrow, shards, steps, spread, step_size,
    bidx_ref, lidx_hbm, scale_hbm, centres_hbm, weights_hbm, pool_hbm, labels_hbm, eig_hbm,
    mt_ref, r_ref,
    lidx, scale, centres, weights, pool, labels, eig,
    w_head, w_rest, e_head, e_rest,
    own_pts, all_pts, x, x_in, ag,
    load_sem, pts_send, pts_recv, x_send, x_recv, ag_send, ag_recv,
):
    me = lax.axis_index("wide") * narrow + lax.axis_index("narrow")
    peers = [lax.rem(me + k, shards) for k in range(1, shards)]

    def at(peer):
        return {"wide": peer // narrow, "narrow": lax.rem(peer, narrow)}

    barrier = pltpu.get_barrier_semaphore()
    for peer in peers:
        pl.semaphore_signal(barrier, inc=1, device_id=at(peer), device_id_type=MESH)

    loads = {}
    for place, (name, src, dst) in enumerate((
        ("pool", pool_hbm, pool),
        ("lidx", lidx_hbm, lidx),
        ("eig", eig_hbm, eig),
        ("centres", centres_hbm, centres),
        ("labels", labels_hbm, labels),
        ("scale", scale_hbm, scale),
        ("weights", weights_hbm, weights),
    )):
        loads[name] = pltpu.make_async_copy(src, dst, load_sem.at[place])
        loads[name].start()

    total = steps * shards
    count, width = centres.shape
    outs = weights.shape[0]
    eigs = eig.shape[0]
    pool_rows = pool.shape[0]
    pieces = width // LANES
    half = x.shape[2]
    w_cols = 2 * half - 256
    b_col = w_cols + eigs - half

    loads["pool"].wait()
    stacked = jnp.concatenate(
        [pool[:, LANES * q:LANES * (q + 1)] for q in range(pieces)], axis=0
    )
    pack_rows = own_pts.shape[0]
    shape = (pack_rows, pieces * pool_rows)
    row, col = iota(shape, 0), iota(shape, 1)
    wanted = row // steps * pool_rows
    step_of = row % steps
    for s in range(steps):
        wanted = wanted + jnp.where(step_of == s, bidx_ref[0, s], 0)
    own = dot(jnp.where(row // steps < pieces, jnp.where(col == wanted, 1.0, 0.0), 0.0).astype(BF16), stacked, NN)
    own_pts[...] = own.astype(BF16)

    pl.semaphore_wait(barrier, shards - 1)
    pts_copies = []
    for peer in peers:
        copy = pltpu.make_async_remote_copy(
            src_ref=own_pts, dst_ref=all_pts.at[me],
            send_sem=pts_send.at[peer], recv_sem=pts_recv.at[me],
            device_id=at(peer), device_id_type=MESH,
        )
        copy.start()
        pts_copies.append(copy)
    all_pts[pl.ds(me, 1)] = own_pts[...][None]
    x[...] = jnp.zeros_like(x)

    loads["lidx"].wait()
    loads["eig"].wait()
    marks = lidx.shape[1]
    chosen = jnp.where(iota((count, marks), 0) == lidx[...], 1.0, 0.0).astype(BF16)
    eig_head, eig_rest = split(eig[...])
    placed = dot(jnp.concatenate([eig_head, eig_rest], axis=0), chosen, NT)
    placed = placed[:eigs] + placed[eigs:]
    e_parts = split(placed)
    e_head[...], e_rest[...] = e_parts

    loads["centres"].wait()
    sums = jnp.zeros((count, LANES), F32)
    for q in range(pieces):
        piece = centres[:, LANES * q:LANES * (q + 1)].astype(F32)
        sums = sums + piece * piece
    s_head, s_rest = split(sums)
    s_tail = (sums - s_head.astype(F32) - s_rest.astype(F32)).astype(BF16)
    ones = jnp.ones((16, LANES), BF16)
    centre_norms = (dot(ones, s_head, NT) + (dot(ones, s_rest, NT) + dot(ones, s_tail, NT)))[0:1]

    loads["labels"].wait()
    shape = (total, pool_rows)
    row, col = iota(shape, 0), iota(shape, 1)
    wanted = jnp.zeros(shape, I32)
    for s in range(steps):
        wanted = wanted + jnp.where(row // shards == s, bidx_ref[0, s], 0)
    pick = jnp.where(row % shards == me, jnp.where(col == wanted, 1.0, 0.0), 0.0).astype(BF16)
    label_rows = dot(pick, labels[...], NN)

    loads["scale"].wait()
    loads["weights"].wait()
    w_parts = split(weights[...])
    w_head[...], w_rest[...] = w_parts

    shape = (pieces * total, shards * pack_rows)
    row, col = iota(shape, 0), iota(shape, 1)
    source = row % shards * pack_rows + row // total * steps + row % total // shards
    order = jnp.where(col == source, 1.0, 0.0).astype(BF16)

    for copy in pts_copies:
        copy.wait_send()
    for peer in peers:
        pltpu.make_async_remote_copy(
            src_ref=own_pts, dst_ref=all_pts.at[peer],
            send_sem=pts_send.at[peer], recv_sem=pts_recv.at[peer],
            device_id=at(peer), device_id_type=MESH,
        ).wait_recv()
    ordered = dot(order, all_pts[...].reshape(shards * pack_rows, LANES), NN)
    points = jnp.concatenate([ordered[total * q:total * (q + 1)] for q in range(pieces)], axis=1)
    point_norms = jnp.sum(points * points, axis=1, keepdims=True)
    dots = dot(points.astype(BF16), centres[...], NT)
    squared = jnp.maximum(centre_norms + point_norms - 2.0 * dots, 0.0)
    kernel = jnp.exp(jnp.sqrt(squared) * (-1.0 / spread))

    k_parts = split(kernel)
    x_w = dot_split(k_parts, (w_head[...], w_rest[...]), NT) - label_rows
    x_e = dot_split(k_parts, (e_head[...], e_rest[...]), NT)
    x_k = dot_split(k_parts, k_parts, NT)
    for s in range(steps):
        rows = slice(shards * s, shards * (s + 1))
        x[2 * s] = x_w[rows, :half]
        x[2 * s + 1, :, :outs - half] = x_w[rows, half:]
        x[2 * s + 1, :, w_cols - half:b_col] = x_e[rows]
        x[2 * s + 1, :, b_col:b_col + total] = x_k[rows]

    x_copies = []
    for peer in peers:
        copy = pltpu.make_async_remote_copy(
            src_ref=x.at[peer], dst_ref=x_in.at[me],
            send_sem=x_send.at[peer], recv_sem=x_recv.at[me],
            device_id=at(peer), device_id_type=MESH,
        )
        copy.start()
        x_copies.append(copy)
    summed = x[pl.ds(me, 1)][0]
    for peer in peers:
        pltpu.make_async_remote_copy(
            src_ref=x.at[peer], dst_ref=x_in.at[peer],
            send_sem=x_send.at[peer], recv_sem=x_recv.at[peer],
            device_id=at(peer), device_id_type=MESH,
        ).wait_recv()
        summed = summed + x_in[pl.ds(peer, 1)][0]
    ag[pl.ds(me, 1)] = summed[None]
    ag_copies = []
    for peer in peers:
        copy = pltpu.make_async_remote_copy(
            src_ref=ag.at[me], dst_ref=ag.at[me],
            send_sem=ag_send.at[peer], recv_sem=ag_recv.at[me],
            device_id=at(peer), device_id_type=MESH,
        )
        copy.start()
        ag_copies.append(copy)
    for copy in x_copies:
        copy.wait_send()
    for peer in peers:
        pltpu.make_async_remote_copy(
            src_ref=ag.at[peer], dst_ref=ag.at[peer],
            send_sem=ag_send.at[peer], recv_sem=ag_recv.at[peer],
            device_id=at(peer), device_id_type=MESH,
        ).wait_recv()
    for copy in ag_copies:
        copy.wait_send()

    left = [ag[2 * s] for s in range(steps)]
    right = [ag[2 * s + 1] for s in range(steps)]
    rights = jnp.concatenate(right, axis=0)
    coeffs = rights[:, w_cols - half:b_col]
    gram = rights[:, b_col:b_col + total]
    scaled = split(coeffs * scale[...])
    coupling = (gram - dot_split(scaled, split(coeffs), NT)) * step_size
    mt_ref[...] = kernel - dot_split(scaled, (e_head[...], e_rest[...]), NN)

    rests = [
        jnp.concatenate([left[s], right[s][:, :w_cols - half]], axis=1) for s in range(steps)
    ]
    for s in range(steps):
        known = rests[s]
        for later in range(s + 1, steps):
            factors = coupling[shards * later:shards * (later + 1), shards * s:shards * (s + 1)]
            moved = rests[later]
            for j in range(shards):
                moved = moved - factors[:, j:j + 1] * known[j:j + 1, :]
            rests[later] = moved
        r_ref[shards * s:shards * (s + 1), :] = known


def apply_kernel(outs, last, mt_ref, r_ref, descent_ref, residual_ref):
    m_head, m_rest = split(mt_ref[...])
    r_all = r_ref[...][:, :outs]
    r_head, r_rest = split(r_all)
    lhs = jnp.concatenate([r_head, r_rest, r_head], axis=0)
    rhs = jnp.concatenate([m_head, m_head, m_rest], axis=0)
    descent_ref[...] = dot(lhs, rhs, TN)
    residual_ref[...] = r_all[last:]


def fused_body(
    narrow, shards,
    centres, weights, pool_points, pool_labels, batch_index, landmark_index, eigvecs, eig_scale
):
    steps = batch_index.shape[0]
    count, width = centres.shape
    outs = weights.shape[1]
    marks, eigs = eigvecs.shape
    pool_rows = pool_points.shape[0]
    spread = math.sqrt(0.5 * width)
    step_size = 32.0 / (count * shards * shards)
    total = steps * shards
    padded = -(-outs // LANES) * LANES
    half = (padded + 256) // 2
    pack_rows = -(-(steps * width // LANES) // 16) * 16
    any_spec = pl.BlockSpec(memory_space=pl.ANY)
    vmem_spec = pl.BlockSpec(memory_space=pltpu.VMEM)
    mt, r = pl.pallas_call(
        functools.partial(steps_kernel, narrow, shards, steps, spread, step_size),
        out_shape=(
            jax.ShapeDtypeStruct((total, count), F32),
            jax.ShapeDtypeStruct((total, padded), F32),
        ),
        in_specs=[pl.BlockSpec(memory_space=pltpu.SMEM)] + [any_spec] * 7,
        out_specs=(vmem_spec, vmem_spec),
        scratch_shapes=[
            pltpu.VMEM((1, marks), I32),
            pltpu.VMEM((1, eigs), F32),
            pltpu.VMEM((count, width), BF16),
            pltpu.VMEM((outs, count), F32),
            pltpu.VMEM((pool_rows, width), BF16),
            pltpu.VMEM((pool_rows, outs), BF16),
            pltpu.VMEM((eigs, marks), F32),
            pltpu.VMEM((outs, count), BF16),
            pltpu.VMEM((outs, count), BF16),
            pltpu.VMEM((eigs, count), BF16),
            pltpu.VMEM((eigs, count), BF16),
            pltpu.VMEM((pack_rows, LANES), BF16),
            pltpu.VMEM((shards, pack_rows, LANES), BF16),
            pltpu.VMEM((shards, ROWS_PER_STEP, half), F32),
            pltpu.VMEM((shards, ROWS_PER_STEP, half), F32),
            pltpu.VMEM((shards, ROWS_PER_STEP, half), F32),
            pltpu.SemaphoreType.DMA((7,)),
        ] + [pltpu.SemaphoreType.DMA((shards,))] * 6,
        compiler_params=pltpu.CompilerParams(
            collective_id=0, has_side_effects=True, vmem_limit_bytes=VMEM_BYTES
        ),
    )(
        batch_index.reshape(1, steps), landmark_index.reshape(1, marks),
        eig_scale.reshape(1, eigs), centres, weights.T, pool_points, pool_labels, eigvecs.T,
    )
    block = count // 3 if count % 384 == 0 else count
    descent, residual = pl.pallas_call(
        functools.partial(apply_kernel, outs, total - shards),
        grid=(count // block,),
        out_shape=(
            jax.ShapeDtypeStruct((outs, count), F32),
            jax.ShapeDtypeStruct((shards, outs), F32),
        ),
        in_specs=[
            pl.BlockSpec((total, block), lambda i: (0, i)),
            pl.BlockSpec((total, padded), lambda i: (0, 0)),
        ],
        out_specs=(
            pl.BlockSpec((outs, block), lambda i: (0, i)),
            pl.BlockSpec((shards, outs), lambda i: (0, 0)),
        ),
        compiler_params=pltpu.CompilerParams(vmem_limit_bytes=VMEM_BYTES),
    )(mt, r)
    return descent.T, residual


def plain_body(
    centres, weights, pool_points, pool_labels, batch_index, landmark_index, eigvecs, eig_scale
):
    axes = ("wide", "narrow")
    shards = lax.axis_size(axes)
    me = lax.axis_index(axes)
    steps, per_device = batch_index.shape
    batch = shards * per_device
    count, width = centres.shape
    outs = weights.shape[1]
    spread = math.sqrt(0.5 * width)
    step_size = 32.0 / (count * shards * batch)
    exact = functools.partial(
        lax.dot_general, precision=lax.Precision.HIGHEST, preferred_element_type=F32
    )
    own_points = jnp.take(pool_points, batch_index, axis=0)
    own_labels = jnp.take(pool_labels, batch_index, axis=0)
    points = lax.all_gather(own_points, axes, axis=1, tiled=True).reshape(steps * batch, width)
    wide_points = points.astype(F32)
    wide_centres = centres.astype(F32)
    point_norms = jnp.sum(wide_points * wide_points, axis=1, keepdims=True)
    centre_norms = jnp.sum(wide_centres * wide_centres, axis=1)[None]
    squared = centre_norms + point_norms - 2.0 * dot(points, centres, NT)
    kernel = jnp.exp(-jnp.sqrt(jnp.maximum(squared, 0.0)) / spread)
    placed = jnp.zeros((count, eigvecs.shape[1]), F32).at[landmark_index].add(eigvecs)
    labels = lax.dynamic_update_slice(
        jnp.zeros((steps, batch, outs), F32), own_labels.astype(F32), (0, me * per_device, 0)
    )
    predicted = exact(kernel, weights, NN) - labels.reshape(steps * batch, outs)
    predicted, coeffs, gram = lax.psum(
        (predicted, exact(kernel, placed, NN), exact(kernel, kernel, NT)), axes
    )
    scaled = coeffs * eig_scale[None]
    coupling = (gram - exact(scaled, coeffs, NT)) * step_size
    mixed = kernel - exact(scaled, placed, NT)
    known = predicted[:batch]
    for s in range(1, steps):
        rows = slice(batch * s, batch * (s + 1))
        fresh = predicted[rows] - exact(coupling[rows, :batch * s], known, NN)
        known = jnp.concatenate([known, fresh], axis=0)
    return exact(mixed, known, TN), known[-batch:]


def solution(mesh):
    narrow = mesh.shape["narrow"]
    shards = mesh.shape["wide"] * narrow

    def body(*args):
        centres, weights = args[0], args[1]
        steps, per_device = args[4].shape
        fits = (
            shards == ROWS_PER_STEP and 2 * steps == shards and per_device == 1
            and centres.shape[1] % LANES == 0 and args[6].shape[1] + steps * shards <= 256
        )
        if fits:
            return fused_body(narrow, shards, *args)
        return plain_body(*args)

    return jax.shard_map(
        body,
        mesh=mesh,
        in_specs=(
            P(("groups", "wide", "narrow"), None),
            P(("groups", "wide", "narrow"), "inner"),
            P(("groups", "wide", "narrow"), None),
            P(("groups", "wide", "narrow"), "inner"),
            P("groups", ("wide", "narrow")),
            P(("groups", "wide", "narrow")),
            P(("groups", "wide", "narrow"), None),
            P("groups"),
        ),
        out_specs=(P(("groups", "wide", "narrow"), "inner"), P("groups", "inner")),
        check_vma=False,
    )
```

```python
import functools
import math

import jax
import jax.numpy as jnp
from jax import lax
from jax.experimental import pallas as pl
from jax.experimental.pallas import tpu as pltpu
from jax.sharding import PartitionSpec as P

MESH = pl.DeviceIdType.MESH
F32, BF16, I32 = jnp.float32, jnp.bfloat16, jnp.int32
LANES = 128
ROWS_PER_STEP = 8
VMEM_BYTES = 56 * 1024 * 1024
APPLY_VMEM_BYTES = 16 * 1024 * 1024

NN = (((1,), (0,)), ((), ()))
NT = (((1,), (1,)), ((), ()))
TN = (((0,), (0,)), ((), ()))


def dot(a, b, dims):
    return lax.dot_general(a, b, dims, preferred_element_type=F32)


def split(x):
    head = x.astype(BF16)
    return head, (x - head.astype(F32)).astype(BF16)


def dot_split(a_parts, b_parts, dims):
    a_head, a_rest = a_parts
    b_head, b_rest = b_parts
    rows = a_head.shape[0]
    both = dot(jnp.concatenate([a_head, a_rest], axis=0), b_head, dims)
    return both[:rows] + (both[rows:] + dot(a_head, b_rest, dims))


def iota(shape, dim):
    return lax.broadcasted_iota(I32, shape, dim)


def steps_kernel(
    narrow, shards, steps, spread, step_size,
    bidx_hbm, lidx_hbm, scale_hbm, centres_hbm, weights_hbm, pool_hbm, labels_hbm, eig_hbm,
    mt_ref, r_ref,
    bidx_ref, lidx, scale, centres, weights, pool, labels, eig,
    w_head, w_rest, e_head, e_rest,
    own_pts, all_pts, ab, ab_in, ab_sum, wx, wx_in, wx_sum,
    load_sem, pts_send, pts_recv, ab_send, ab_recv, ab_out, ab_back, wx_send, wx_recv, wx_out, wx_back,
):
    me = lax.axis_index("wide") * narrow + lax.axis_index("narrow")
    peers = [lax.rem(me + k, shards) for k in range(1, shards)]

    def at(peer):
        return {"wide": peer // narrow, "narrow": lax.rem(peer, narrow)}

    def remote(src, dst, send, recv, peer, slot):
        return pltpu.make_async_remote_copy(
            src_ref=src, dst_ref=dst.at[slot], send_sem=send.at[peer], recv_sem=recv.at[slot],
            device_id=at(peer), device_id_type=MESH,
        )

    def send_each(src_of, dst, send, recv):
        copies = [remote(src_of(peer), dst, send, recv, peer, me) for peer in peers]
        for copy in copies:
            copy.start()
        return copies

    def wait_each(src_of, dst, send, recv):
        for peer in peers:
            remote(src_of(peer), dst, send, recv, peer, peer).wait_recv()

    def added(own, slots):
        terms = [own[pl.ds(me, 1)][0]] + [slots[pl.ds(peer, 1)][0] for peer in peers]
        while len(terms) > 1:
            terms = [sum(terms[k:k + 2][1:], terms[k]) for k in range(0, len(terms), 2)]
        return terms[0]

    barrier = pltpu.get_barrier_semaphore()
    for peer in peers:
        pl.semaphore_signal(barrier, inc=1, device_id=at(peer), device_id_type=MESH)

    loads = {}
    for place, (name, src, dst) in enumerate((
        ("bidx", bidx_hbm, bidx_ref),
        ("pool", pool_hbm, pool),
        ("lidx", lidx_hbm, lidx),
        ("eig", eig_hbm, eig),
        ("centres", centres_hbm, centres),
        ("labels", labels_hbm, labels),
        ("scale", scale_hbm, scale),
        ("weights", weights_hbm, weights),
    )):
        loads[name] = pltpu.make_async_copy(src, dst, load_sem.at[place])
        loads[name].start()

    total = steps * shards
    count, width = centres.shape
    outs = weights.shape[0]
    eigs = eig.shape[0]
    pool_rows = pool.shape[0]
    pieces = width // LANES
    w_half, ab_half = wx.shape[2], ab.shape[2]

    loads["pool"].wait()
    loads["bidx"].wait()
    stacked = jnp.concatenate(
        [pool[:, LANES * q:LANES * (q + 1)] for q in range(pieces)], axis=0
    )
    pack_rows = own_pts.shape[0]
    shape = (pack_rows, pieces * pool_rows)
    row, col = iota(shape, 0), iota(shape, 1)
    wanted = row // steps * pool_rows
    step_of = row % steps
    for s in range(steps):
        wanted = wanted + jnp.where(step_of == s, bidx_ref[0, s], 0)
    own = dot(jnp.where(row // steps < pieces, jnp.where(col == wanted, 1.0, 0.0), 0.0).astype(BF16), stacked, NN)
    own_pts[...] = own.astype(BF16)

    pl.semaphore_wait(barrier, shards - 1)
    copies = send_each(lambda peer: own_pts, all_pts, pts_send, pts_recv)
    all_pts[pl.ds(me, 1)] = own_pts[...][None]
    ab[...] = jnp.zeros_like(ab)
    wx[...] = jnp.zeros_like(wx)

    loads["lidx"].wait()
    loads["eig"].wait()
    marks = lidx.shape[1]
    chosen = jnp.where(iota((count, marks), 0) == lidx[...], 1.0, 0.0).astype(BF16)
    eig_head, eig_rest = split(eig[...])
    placed = dot(jnp.concatenate([eig_head, eig_rest], axis=0), chosen, NT)
    placed = placed[:eigs] + placed[eigs:]
    e_parts = split(placed)
    e_head[...], e_rest[...] = e_parts

    loads["centres"].wait()
    sums = jnp.zeros((count, LANES), F32)
    for q in range(pieces):
        piece = centres[:, LANES * q:LANES * (q + 1)].astype(F32)
        sums = sums + piece * piece
    s_head, s_rest = split(sums)
    s_tail = (sums - s_head.astype(F32) - s_rest.astype(F32)).astype(BF16)
    ones = jnp.ones((16, LANES), BF16)
    centre_norms = (dot(ones, s_head, NT) + (dot(ones, s_rest, NT) + dot(ones, s_tail, NT)))[0:1]

    loads["labels"].wait()
    shape = (total, pool_rows)
    row, col = iota(shape, 0), iota(shape, 1)
    wanted = jnp.zeros(shape, I32)
    for s in range(steps):
        wanted = wanted + jnp.where(row // shards == s, bidx_ref[0, s], 0)
    pick = jnp.where(row % shards == me, jnp.where(col == wanted, 1.0, 0.0), 0.0).astype(BF16)
    label_rows = dot(pick, labels[...], NN)

    loads["scale"].wait()
    loads["weights"].wait()
    w_parts = split(weights[...])
    w_head[...], w_rest[...] = w_parts

    shape = (pieces * total, shards * pack_rows)
    row, col = iota(shape, 0), iota(shape, 1)
    source = row % shards * pack_rows + row // total * steps + row % total // shards
    order = jnp.where(col == source, 1.0, 0.0).astype(BF16)

    wait_each(lambda peer: own_pts, all_pts, pts_send, pts_recv)
    ordered = dot(order, all_pts[...].reshape(shards * pack_rows, LANES), NN)
    points = jnp.concatenate([ordered[total * q:total * (q + 1)] for q in range(pieces)], axis=1)
    point_norms = jnp.sum(points * points, axis=1, keepdims=True)
    dots = dot(points.astype(BF16), centres[...], NT)
    squared = jnp.maximum(centre_norms + point_norms - 2.0 * dots, 0.0)
    kernel = jnp.exp(jnp.sqrt(squared) * (-1.0 / spread))

    k_parts = split(kernel)
    x_e = dot_split(k_parts, (e_head[...], e_rest[...]), NT)
    x_k = dot_split(k_parts, k_parts, NT)
    for s in range(steps):
        rows = slice(shards * s, shards * (s + 1))
        ab[2 * s] = x_e[rows, :ab_half]
        ab[2 * s + 1, :, :eigs - ab_half] = x_e[rows, ab_half:]
        ab[2 * s + 1, :, eigs - ab_half:eigs - ab_half + total] = x_k[rows]
    copies += send_each(lambda peer: ab.at[peer], ab_in, ab_send, ab_recv)

    x_w = dot_split(k_parts, (w_head[...], w_rest[...]), NT) - label_rows
    for s in range(steps):
        rows = slice(shards * s, shards * (s + 1))
        wx[2 * s] = x_w[rows, :w_half]
        wx[2 * s + 1, :, :outs - w_half] = x_w[rows, w_half:]
    copies += send_each(lambda peer: wx.at[peer], wx_in, wx_send, wx_recv)

    wait_each(lambda peer: ab.at[peer], ab_in, ab_send, ab_recv)
    ab_sum[pl.ds(me, 1)] = added(ab, ab_in)[None]
    copies += send_each(lambda peer: ab_sum.at[me], ab_sum, ab_out, ab_back)

    wait_each(lambda peer: wx.at[peer], wx_in, wx_send, wx_recv)
    wx_sum[pl.ds(me, 1)] = added(wx, wx_in)[None]
    copies += send_each(lambda peer: wx_sum.at[me], wx_sum, wx_out, wx_back)

    wait_each(lambda peer: ab_sum.at[peer], ab_sum, ab_out, ab_back)
    both = jnp.concatenate(
        [jnp.concatenate([ab_sum[2 * s], ab_sum[2 * s + 1]], axis=1) for s in range(steps)], axis=0
    )
    coeffs = both[:, :eigs]
    gram = both[:, eigs:eigs + total]
    scaled = split(coeffs * scale[...])
    coupling = (gram - dot_split(scaled, split(coeffs), NT)) * step_size
    mt_ref[...] = kernel - dot_split(scaled, (e_head[...], e_rest[...]), NN)

    wait_each(lambda peer: wx_sum.at[peer], wx_sum, wx_out, wx_back)
    rests = [jnp.concatenate([wx_sum[2 * s], wx_sum[2 * s + 1]], axis=1) for s in range(steps)]
    for s in range(steps):
        known = rests[s]
        for later in range(s + 1, steps):
            factors = coupling[shards * later:shards * (later + 1), shards * s:shards * (s + 1)]
            moved = rests[later]
            for j in range(shards):
                moved = moved - factors[:, j:j + 1] * known[j:j + 1, :]
            rests[later] = moved
        r_ref[shards * s:shards * (s + 1), :] = known
    for copy in copies:
        copy.wait_send()


def apply_kernel(outs, last, mt_ref, r_ref, descent_ref, residual_ref):
    m_head, m_rest = split(mt_ref[...])
    r_all = r_ref[...][:, :outs]
    r_head, r_rest = split(r_all)
    lhs = jnp.concatenate([r_head, r_rest, r_head], axis=0)
    rhs = jnp.concatenate([m_head, m_head, m_rest], axis=0)
    descent_ref[...] = dot(lhs, rhs, TN)
    residual_ref[...] = r_all[last:]


def fused_body(
    narrow, shards,
    centres, weights, pool_points, pool_labels, batch_index, landmark_index, eigvecs, eig_scale
):
    steps = batch_index.shape[0]
    count, width = centres.shape
    outs = weights.shape[1]
    marks, eigs = eigvecs.shape
    pool_rows = pool_points.shape[0]
    spread = math.sqrt(0.5 * width)
    step_size = 32.0 / (count * shards * shards)
    total = steps * shards
    padded = -(-outs // (2 * LANES)) * 2 * LANES
    pack_rows = -(-(steps * width // LANES) // 16) * 16
    vmem_spec = pl.BlockSpec(memory_space=pltpu.VMEM)
    mt, r = pl.pallas_call(
        functools.partial(steps_kernel, narrow, shards, steps, spread, step_size),
        out_shape=(
            pltpu.VMEM((total, count), F32),
            pltpu.VMEM((total, padded), F32),
        ),
        in_specs=[pl.BlockSpec(memory_space=pltpu.HBM)] * 8,
        out_specs=(vmem_spec, vmem_spec),
        scratch_shapes=[
            pltpu.SMEM((1, steps), I32),
            pltpu.VMEM((1, marks), I32),
            pltpu.VMEM((1, eigs), F32),
            pltpu.VMEM((count, width), BF16),
            pltpu.VMEM((outs, count), F32),
            pltpu.VMEM((pool_rows, width), BF16),
            pltpu.VMEM((pool_rows, outs), BF16),
            pltpu.VMEM((eigs, marks), F32),
            pltpu.VMEM((outs, count), BF16),
            pltpu.VMEM((outs, count), BF16),
            pltpu.VMEM((eigs, count), BF16),
            pltpu.VMEM((eigs, count), BF16),
            pltpu.VMEM((pack_rows, LANES), BF16),
            pltpu.VMEM((shards, pack_rows, LANES), BF16),
        ] + [pltpu.VMEM((shards, ROWS_PER_STEP, LANES), F32)] * 3
        + [pltpu.VMEM((shards, ROWS_PER_STEP, padded // 2), F32)] * 3
        + [pltpu.SemaphoreType.DMA((8,))]
        + [pltpu.SemaphoreType.DMA((shards,))] * 10,
        compiler_params=pltpu.CompilerParams(
            collective_id=0, has_side_effects=True, vmem_limit_bytes=VMEM_BYTES
        ),
    )(
        batch_index.reshape(1, steps), landmark_index.reshape(1, marks),
        eig_scale.reshape(1, eigs), centres, weights.T, pool_points, pool_labels, eigvecs.T,
    )
    block = count // 3 if count % 384 == 0 else count
    descent, residual = pl.pallas_call(
        functools.partial(apply_kernel, outs, total - shards),
        grid=(count // block,),
        out_shape=(
            jax.ShapeDtypeStruct((outs, count), F32),
            jax.ShapeDtypeStruct((shards, outs), F32),
        ),
        in_specs=[
            pl.BlockSpec((total, block), lambda i: (0, i)),
            pl.BlockSpec((total, padded), lambda i: (0, 0)),
        ],
        out_specs=(
            pl.BlockSpec((outs, block), lambda i: (0, i)),
            pl.BlockSpec((shards, outs), lambda i: (0, 0)),
        ),
        compiler_params=pltpu.CompilerParams(vmem_limit_bytes=APPLY_VMEM_BYTES),
    )(mt, r)
    return descent.T, residual


def plain_body(
    centres, weights, pool_points, pool_labels, batch_index, landmark_index, eigvecs, eig_scale
):
    axes = ("wide", "narrow")
    shards = lax.axis_size(axes)
    me = lax.axis_index(axes)
    steps, per_device = batch_index.shape
    batch = shards * per_device
    count, width = centres.shape
    outs = weights.shape[1]
    spread = math.sqrt(0.5 * width)
    step_size = 32.0 / (count * shards * batch)
    exact = functools.partial(
        lax.dot_general, precision=lax.Precision.HIGHEST, preferred_element_type=F32
    )
    own_points = jnp.take(pool_points, batch_index, axis=0)
    own_labels = jnp.take(pool_labels, batch_index, axis=0)
    points = lax.all_gather(own_points, axes, axis=1, tiled=True).reshape(steps * batch, width)
    wide_points = points.astype(F32)
    wide_centres = centres.astype(F32)
    point_norms = jnp.sum(wide_points * wide_points, axis=1, keepdims=True)
    centre_norms = jnp.sum(wide_centres * wide_centres, axis=1)[None]
    squared = centre_norms + point_norms - 2.0 * dot(points, centres, NT)
    kernel = jnp.exp(-jnp.sqrt(jnp.maximum(squared, 0.0)) / spread)
    placed = jnp.zeros((count, eigvecs.shape[1]), F32).at[landmark_index].add(eigvecs)
    labels = lax.dynamic_update_slice(
        jnp.zeros((steps, batch, outs), F32), own_labels.astype(F32), (0, me * per_device, 0)
    )
    predicted = exact(kernel, weights, NN) - labels.reshape(steps * batch, outs)
    predicted, coeffs, gram = lax.psum(
        (predicted, exact(kernel, placed, NN), exact(kernel, kernel, NT)), axes
    )
    scaled = coeffs * eig_scale[None]
    coupling = (gram - exact(scaled, coeffs, NT)) * step_size
    mixed = kernel - exact(scaled, placed, NT)
    known = predicted[:batch]
    for s in range(1, steps):
        rows = slice(batch * s, batch * (s + 1))
        fresh = predicted[rows] - exact(coupling[rows, :batch * s], known, NN)
        known = jnp.concatenate([known, fresh], axis=0)
    return exact(mixed, known, TN), known[-batch:]


def solution(mesh):
    narrow = mesh.shape["narrow"]
    shards = mesh.shape["wide"] * narrow

    def body(*args):
        centres, weights = args[0], args[1]
        steps, per_device = args[4].shape
        fits = (
            shards == ROWS_PER_STEP and 2 * steps == shards and per_device == 1
            and centres.shape[1] % LANES == 0 and args[6].shape[1] + steps * shards <= 256
        )
        if fits:
            return fused_body(narrow, shards, *args)
        return plain_body(*args)

    return jax.shard_map(
        body,
        mesh=mesh,
        in_specs=(
            P(("groups", "wide", "narrow"), None),
            P(("groups", "wide", "narrow"), "inner"),
            P(("groups", "wide", "narrow"), None),
            P(("groups", "wide", "narrow"), "inner"),
            P("groups", ("wide", "narrow")),
            P(("groups", "wide", "narrow")),
            P(("groups", "wide", "narrow"), None),
            P("groups"),
        ),
        out_specs=(P(("groups", "wide", "narrow"), "inner"), P("groups", "inner")),
        check_vma=False,
    )
```
